32 devices in a mesh: tok: 16 (over z, x, core), head: 2 (over y).
Axes of the slice: x: 2, y: 2, z: 4, core: 2. Of those that a mesh axis runs over, the one named last changes fastest.
Arguments:
- queries: bfloat16 [2, 2, 4096, 8192], P(None, None, 'tok', 'head'), may hold values from -6 to 6
- first_keys: bfloat16 [2, 4096, 8192], P(None, 'tok', 'head'), may hold values from -6 to 6
- first_values: bfloat16 [2, 4096, 8192], P(None, 'tok', 'head'), may hold values from -6 to 6
- first_rates: float32 [2, 16, 4096], P(None, 'head', 'tok'), may hold values from 0.1 to 1
- w_one: bfloat16 [16, 512, 512], P('head'), may hold values from -0.25 to 0.25
- w_three: bfloat16 [16, 512, 512], P('head'), may hold values from -0.25 to 0.25
- w_two: bfloat16 [16, 512, 512], P('head'), may hold values from -0.25 to 0.25
- step_size: float32 [16], P('head'), may hold values from 0.02 to 0.06
- out_gain: float32 [8192], replicated, may hold values from 0.25 to 1.75
Outputs:
- normed_rows: bfloat16 [2, 2, 4096, 8192], P(None, None, ('tok', 'head'))
The draws below stay inside these ranges and needn't reach their ends.
All inputs are finite; a program needn't handle non-finite values.
Results may differ from the reference program's by a relative error of at most 0.025.
Values may be sent and summed in bfloat16 or wider, within the bound.
A program may use at most 192 MiB of HBM per device.

```python
import math
import jax
import jax.numpy as jnp
from jax import lax

HEADS = 16
HD = 512
HH = 512
SEQS = 2
GROUPS = 2
CTOK = 256
GROUP = 4096
WIDTH = 8192
N_TOK = 16


def levels(own_key, extent, cuts, smallest, top_value):
    def one(dim, blocks):
        draws = jax.random.uniform(jax.random.fold_in(jax.random.fold_in(own_key, 6), dim), (blocks,), jnp.float32, smallest / len(cuts), top_value / len(cuts))
        return jnp.repeat(jnp.exp(draws), extent[dim] // blocks).reshape((-1,) + (1,) * (len(extent) - dim - 1))

    level = one(*cuts[0])
    for cut in cuts[1:]:
        level = level * one(*cut)
    return level


def bell_draw(stream_key, extent, spread, reach, shards=(), kind=jnp.bfloat16):
    level = levels(stream_key, extent, shards, -0.22, 0.18) if shards else 1.0
    drawn = jax.random.normal(stream_key, extent, jnp.float32) * spread * level
    return jnp.minimum(jnp.maximum(drawn, -reach), reach).astype(kind)


def setup_inputs(seed: int = 0) -> dict:
    splits = jax.random.split(jax.random.key(seed), 10)
    return {
        "queries": bell_draw(splits[0], (SEQS, GROUPS, GROUP, WIDTH), 1.0, 6.0, ((2, 16), (3, 2))),
        "first_keys": bell_draw(splits[1], (SEQS, GROUP, WIDTH), 1.0, 6.0, ((1, 16), (2, 2))),
        "first_values": bell_draw(splits[2], (SEQS, GROUP, WIDTH), 1.0, 6.0, ((1, 16), (2, 2))),
        "first_rates": jnp.clip(jnp.exp(math.log(1.0) - 2.3025851 * jax.random.uniform(splits[3], (SEQS, HEADS, GROUP), jnp.float32) ** levels(splits[3], (SEQS, HEADS, GROUP), ((1, 2), (2, 16)), -0.2, 0.2)), 0.1, 1.0),
        "w_one": bell_draw(splits[4], (HEADS, HD, HH), HD ** -0.5, 0.25, ((0, 2),)),
        "w_three": bell_draw(splits[5], (HEADS, HD, HH), HD ** -0.5, 0.25, ((0, 2),)),
        "w_two": bell_draw(splits[6], (HEADS, HH, HD), HH ** -0.5, 0.25, ((0, 2),)),
        "step_size": jnp.clip(jnp.exp(math.log(0.06) - 1.0986123 * jax.random.uniform(splits[7], (HEADS,), jnp.float32) ** levels(splits[7], (HEADS,), ((0, 2),), -0.2, 0.2)), 0.02, 0.06),
        "out_gain": jnp.clip(1.0 + 0.15 * jax.random.normal(splits[8], (WIDTH,), jnp.float32), 0.25, 1.75),
    }


def swiglu_apply(inputs, w_one, w_three, w_two):
    gate_pre = jnp.einsum('...a,ab->...b', inputs.astype(jnp.float32), w_one.astype(jnp.float32))
    up_pre = jnp.einsum('...a,ab->...b', inputs.astype(jnp.float32), w_three.astype(jnp.float32))
    hidden = (gate_pre * jax.nn.sigmoid(gate_pre) * up_pre).astype(jnp.bfloat16)
    result = jnp.einsum('...b,ba->...a', hidden.astype(jnp.float32), w_two.astype(jnp.float32))
    return result.astype(jnp.bfloat16)

def block_sum(left, right):
    left_blocks = left.reshape(N_TOK, CTOK, left.shape[-1]).astype(jnp.float32)
    right_blocks = right.reshape(N_TOK, CTOK, right.shape[-1]).astype(jnp.float32)
    partials = jnp.einsum('nta,ntb->nab', left_blocks, right_blocks)
    rounded = lax.optimization_barrier(partials.astype(jnp.bfloat16))
    return lax.optimization_barrier(jnp.sum(rounded.astype(jnp.float32), axis=0))

def head_gradient(keys_head, values_head, rates_head, w_one, w_three, w_two):
    gate_pre = jnp.dot(keys_head, w_one, preferred_element_type=jnp.float32)
    up_pre = jnp.dot(keys_head, w_three, preferred_element_type=jnp.float32)
    sigma = jax.nn.sigmoid(gate_pre)
    hidden = (gate_pre * sigma * up_pre).astype(jnp.bfloat16)
    scaled = (-rates_head[:, None] * values_head.astype(jnp.float32)).astype(jnp.bfloat16)
    back = jnp.dot(scaled, w_two.T, preferred_element_type=jnp.float32)
    d_up = (back * gate_pre * sigma).astype(jnp.bfloat16)
    d_gate = (back * up_pre * sigma * (1.0 + gate_pre * (1.0 - sigma))).astype(jnp.bfloat16)
    grad_one = block_sum(keys_head, d_gate)
    grad_three = block_sum(keys_head, d_up)
    grad_two = block_sum(hidden, scaled)
    return (grad_one, grad_three, grad_two)

def renew(weight, grad, rate):
    mean_sq = jnp.mean(grad * grad)
    return (weight.astype(jnp.float32) - rate * grad * lax.rsqrt(mean_sq + 1e-05)).astype(jnp.bfloat16)

def per_head(operands):
    query_head, keys_head, values_head, rates_head, w_one, w_three, w_two, rate = operands
    results = []
    for sequence in range(SEQS):
        first = swiglu_apply(query_head[sequence, 0], w_one, w_three, w_two)
        grad_one, grad_three, grad_two = head_gradient(keys_head[sequence], values_head[sequence], rates_head[sequence], w_one, w_three, w_two)
        new_one = renew(w_one, grad_one, rate)
        new_three = renew(w_three, grad_three, rate)
        new_two = renew(w_two, grad_two, rate)
        second = swiglu_apply(query_head[sequence, 1], new_one, new_three, new_two)
        results.append(jnp.stack([first, second]))
    return jnp.stack(results)

def reference(queries, first_keys, first_values, first_rates, w_one, w_three, w_two, step_size, out_gain):
    query_heads = jnp.moveaxis(queries.reshape(SEQS, GROUPS, GROUP, HEADS, HD), 3, 0)
    key_heads = jnp.moveaxis(first_keys.reshape(SEQS, GROUP, HEADS, HD), 2, 0)
    value_heads = jnp.moveaxis(first_values.reshape(SEQS, GROUP, HEADS, HD), 2, 0)
    rate_heads = jnp.moveaxis(first_rates, 1, 0)
    outputs = lax.map(per_head, (query_heads, key_heads, value_heads, rate_heads, w_one, w_three, w_two, step_size))
    merged = jnp.moveaxis(outputs, 0, 3).reshape(SEQS, GROUPS, GROUP, WIDTH).astype(jnp.float32)
    mean_sq = lax.optimization_barrier(jnp.mean(merged * merged, axis=-1, keepdims=True))
    return (merged * lax.rsqrt(mean_sq + 1e-06) * out_gain).astype(jnp.bfloat16)
```

```python
import functools

import jax
import jax.numpy as jnp
from jax import lax
from jax.experimental import pallas as pl
from jax.experimental.pallas import tpu as pltpu
from jax.sharding import PartitionSpec as P

MESH = pl.DeviceIdType.MESH
F32 = jnp.float32
BF16 = jnp.bfloat16


def dot(left, right):
    return jnp.dot(left, right, preferred_element_type=F32)


def dot_tn(left, right):
    return lax.dot_general(left, right, (((0,), (0,)), ((), ())), preferred_element_type=F32)


def dot_nt(left, right):
    return lax.dot_general(left, right, (((1,), (1,)), ((), ())), preferred_element_type=F32)


def fast_map(rows, one, three, two):
    gate = dot(rows, one)
    up = dot(rows, three)
    hidden = (gate * jax.nn.sigmoid(gate) * up).astype(BF16)
    return dot(hidden, two).astype(BF16)


def kernel(
    dims,
    queries, keys, scaled, w_one, w_three, w_two, step_size, gain,
    out,
    k_buf, s_buf, q_buf, w_slot, x_slot, own_w, first_buf, second_buf, rows_buf,
    grads, sent, received, renewed,
    slot_sem, own_sem, local_sem, tok_send, tok_recv, first_send, first_recv,
    ex_send, ex_recv, second_send, second_recv, out_sem,
):
    n_tok, n_head, seqs, heads, rows, hd = dims
    members = heads
    steps = (n_tok // members).bit_length() - 1
    sub = rows // n_head
    here = heads * hd
    tok, head = lax.axis_index("tok"), lax.axis_index("head")
    g = lax.rem(tok, members)
    base = tok - g
    rank = lax.div(tok, members)

    def member(j):
        return lax.rem(g + j, members)

    def peer_head(k):
        return lax.rem(head + k, n_head)

    def partner(step):
        bit = 1 << step
        side = lax.rem(lax.div(rank, bit), 2)
        return (rank + bit * (1 - 2 * side)) * members + g

    def cols(index):
        return pl.ds(pl.multiple_of(index * hd, hd), hd)

    def block(index):
        return pl.ds(pl.multiple_of(index * rows, rows), rows)

    barrier = pltpu.get_barrier_semaphore()
    count = 0
    for j in range(members):
        for k in range(n_head):
            if j or k:
                pl.semaphore_signal(
                    barrier, inc=1, device_id=(base + member(j), peer_head(k)), device_id_type=MESH
                )
                count += 1
    for step in range(steps):
        pl.semaphore_signal(
            barrier, inc=1, device_id=(partner(step), head), device_id_type=MESH
        )
        count += 1
    pl.semaphore_wait(barrier, count)

    def token_parts(kind, s, peer):
        source = (keys.at[s], scaled.at[s], queries.at[s, 1])[kind]
        target = (k_buf, s_buf, q_buf)[kind]
        return source.at[:, cols(peer)], target.at[s, block(g), :]

    def token_copy(kind, s, j):
        peer = member(j)
        src, dst = token_parts(kind, s, peer)
        return pltpu.make_async_remote_copy(
            src_ref=src, dst_ref=dst,
            send_sem=tok_send.at[kind, s, j], recv_sem=tok_recv.at[kind, s, j],
            device_id=(base + peer, head), device_id_type=MESH,
        )

    def token_local(kind, s):
        src, dst = token_parts(kind, s, g)
        return pltpu.make_async_copy(src, dst, local_sem.at[kind, s])

    def start_tokens(kinds, s):
        def body(j, carry):
            for kind in kinds:
                token_copy(kind, s, j).start()
            return carry

        lax.fori_loop(1, members, body, 0)
        for kind in kinds:
            token_local(kind, s).start()

    own_copies = [
        pltpu.make_async_copy(w.at[g], own_w.at[i], own_sem.at[i])
        for i, w in enumerate((w_one, w_three, w_two))
    ]
    for s in range(seqs):
        start_tokens((0, 1), s)
    for copy in own_copies:
        copy.start()

    def fetch(h, slot):
        copies = [
            pltpu.make_async_copy(w.at[h], w_slot.at[slot, i], slot_sem.at[slot, i])
            for i, w in enumerate((w_one, w_three, w_two))
        ]
        for s in range(seqs):
            copies.append(
                pltpu.make_async_copy(
                    queries.at[s, 0, :, cols(h)],
                    x_slot.at[slot, pl.ds(s * rows, rows), :],
                    slot_sem.at[slot, 3 + s],
                )
            )
        return copies

    def first_copy(h, s, k):
        dest = peer_head(k)
        return pltpu.make_async_remote_copy(
            src_ref=first_buf.at[h, pl.ds(pl.multiple_of(s * rows + dest * sub, sub), sub), :],
            dst_ref=rows_buf.at[s, 0, :, cols(head * heads + h)],
            send_sem=first_send.at[h, s, k], recv_sem=first_recv.at[h, s, k],
            device_id=(tok, dest), device_id_type=MESH,
        )

    for copy in fetch(0, 0):
        copy.start()

    def first_body(h, carry):
        slot = lax.rem(h, 2)

        @pl.when(h + 1 < heads)
        def _():
            for copy in fetch(h + 1, lax.rem(h + 1, 2)):
                copy.start()

        for copy in fetch(h, slot):
            copy.wait()
        first_buf[h] = fast_map(x_slot[slot], w_slot[slot, 0], w_slot[slot, 1], w_slot[slot, 2])
        for s in range(seqs):
            for k in range(1, n_head):
                first_copy(h, s, k).start()
            rows_buf[s, 0, :, cols(head * heads + h)] = first_buf[
                h, pl.ds(pl.multiple_of(s * rows + head * sub, sub), sub), :
            ]
        return carry

    lax.fori_loop(0, heads, first_body, 0)
    for copy in own_copies:
        copy.wait()

    def add_block(s, b):
        key_rows = k_buf[s, block(b), :]
        scaled_rows = s_buf[s, block(b), :]
        gate = dot(key_rows, own_w[0])
        up = dot(key_rows, own_w[1])
        back = dot_nt(scaled_rows, own_w[2])
        sig = jax.nn.sigmoid(gate)
        swish = gate * sig
        hidden = (swish * up).astype(BF16)
        d_up = (back * swish).astype(BF16)
        d_gate = (back * up * sig * (1.0 + gate * (1.0 - sig))).astype(BF16)
        grads[s, 0] += dot_tn(key_rows, d_gate)
        grads[s, 1] += dot_tn(key_rows, d_up)
        grads[s, 2] += dot_tn(hidden, scaled_rows)

    def exchange(s, step):
        return pltpu.make_async_remote_copy(
            src_ref=sent.at[s, step], dst_ref=received.at[s, step],
            send_sem=ex_send.at[s, step], recv_sem=ex_recv.at[s, step],
            device_id=(partner(step), head), device_id_type=MESH,
        )

    def start_exchange(s, step):
        sent[s, step] = grads[s].astype(BF16)
        exchange(s, step).start()

    for s in range(seqs):
        grads[s] = jnp.zeros_like(grads[s])
        for kind in (0, 1):
            token_local(kind, s).wait()
        add_block(s, g)

        def grad_body(j, carry):
            for kind in (0, 1):
                token_copy(kind, s, j).wait_recv()
            add_block(s, lax.rem(g + members - j, members))
            return carry

        lax.fori_loop(1, members, grad_body, 0)
        if steps:
            start_exchange(s, 0)
        start_tokens((2,), s)

    tile = 16

    def normalize(s, group):
        def body(r, carry):
            at = pl.ds(pl.multiple_of(r * tile, tile), tile)
            values = rows_buf[s, group, at, :].astype(F32)
            mean_sq = jnp.mean(values * values, axis=-1, keepdims=True)
            rows_buf[s, group, at, :] = (
                values * lax.rsqrt(mean_sq + 1e-06) * gain[...]
            ).astype(BF16)
            return carry

        lax.fori_loop(0, sub // tile, body, 0)
        out_copy(s, group).start()

    def out_copy(s, group):
        return pltpu.make_async_copy(
            rows_buf.at[s, group], out.at[s, group], out_sem.at[s, group]
        )

    def wait_first(h, carry):
        for s in range(seqs):
            for k in range(1, n_head):
                first_copy(h, s, k).wait()
        return carry

    lax.fori_loop(0, heads, wait_first, 0)
    for s in range(seqs):
        normalize(s, 0)

    def second_copy(s, j, k):
        b, dest = member(j), peer_head(k)
        return pltpu.make_async_remote_copy(
            src_ref=second_buf.at[
                s, pl.ds(pl.multiple_of(b * rows + dest * sub, sub), sub), :
            ],
            dst_ref=rows_buf.at[s, 1, :, cols(head * heads + g)],
            send_sem=second_send.at[s, j, k], recv_sem=second_recv.at[s, j, k],
            device_id=(base + b, dest), device_id_type=MESH,
        )

    rate = step_size[g]
    for s in range(seqs):
        for step in range(steps):
            exchange(s, step).wait()
            grads[s] += received[s, step].astype(F32)
            if step + 1 < steps:
                start_exchange(s, step + 1)
        for i in range(3):
            total = grads[s, i]
            mean_sq = jnp.mean(
                jnp.mean(total * total, axis=0, keepdims=True), axis=1, keepdims=True
            )
            renewed[i] = (
                own_w[i].astype(F32) - rate * total * lax.rsqrt(mean_sq + 1e-05)
            ).astype(BF16)

        def wait_queries(j, carry):
            token_copy(2, s, j).wait_recv()
            return carry

        lax.fori_loop(1, members, wait_queries, 0)
        token_local(2, s).wait()

        def second_block(b):
            second_buf[s, block(b), :] = fast_map(
                q_buf[s, block(b), :], renewed[0], renewed[1], renewed[2]
            )

        def second_body(j, carry):
            second_block(member(j))
            for k in range(n_head):
                second_copy(s, j, k).start()
            return carry

        lax.fori_loop(1, members, second_body, 0)
        second_block(g)
        for k in range(1, n_head):
            second_copy(s, 0, k).start()
        rows_buf[s, 1, :, cols(head * heads + g)] = second_buf[
            s, pl.ds(pl.multiple_of(g * rows + head * sub, sub), sub), :
        ]

    for s in range(seqs):
        for k in range(1, n_head):
            second_copy(s, 0, k).wait()

        def wait_second(j, carry):
            for k in range(n_head):
                second_copy(s, j, k).wait()
            return carry

        lax.fori_loop(1, members, wait_second, 0)
        normalize(s, 1)

    def drain(j, carry):
        for s in range(seqs):
            for kind in range(3):
                token_copy(kind, s, j).wait_send()
        return carry

    lax.fori_loop(1, members, drain, 0)
    for s in range(seqs):
        for group in range(2):
            out_copy(s, group).wait()


def solution(mesh):
    n_tok, n_head = mesh.shape["tok"], mesh.shape["head"]

    def shards(
        queries, first_keys, first_values, first_rates, w_one, w_three, w_two, step_size, out_gain
    ):
        seqs, groups, rows, here = queries.shape
        heads, hd, hh = w_one.shape
        members = heads
        steps = (n_tok // members).bit_length() - 1
        sub = rows // n_head
        width = here * n_head
        values = first_values.reshape(seqs, rows, heads, hd).astype(F32)
        rates = jnp.transpose(first_rates, (0, 2, 1))[..., None]
        scaled = (-rates * values).astype(BF16).reshape(first_values.shape)
        anywhere = pl.BlockSpec(memory_space=pl.ANY)
        vmem = pl.BlockSpec(memory_space=pltpu.VMEM)
        smem = pl.BlockSpec(memory_space=pltpu.SMEM)
        sem = pltpu.SemaphoreType.DMA
        dims = (n_tok, n_head, seqs, heads, rows, hd)
        group_rows = members * rows
        flops = 24 * seqs * heads * rows * hd * hh
        return pl.pallas_call(
            functools.partial(kernel, dims),
            out_shape=jax.ShapeDtypeStruct((seqs, groups, sub, width), BF16),
            in_specs=[anywhere] * 6 + [smem, vmem],
            out_specs=anywhere,
            scratch_shapes=[
                pltpu.VMEM((seqs, group_rows, hd), BF16),
                pltpu.VMEM((seqs, group_rows, hd), BF16),
                pltpu.VMEM((seqs, group_rows, hd), BF16),
                pltpu.VMEM((2, 3, hd, hh), BF16),
                pltpu.VMEM((2, seqs * rows, hd), BF16),
                pltpu.VMEM((3, hd, hh), BF16),
                pltpu.VMEM((heads, seqs * rows, hd), BF16),
                pltpu.VMEM((seqs, group_rows, hd), BF16),
                pltpu.VMEM((seqs, groups, sub, width), BF16),
                pltpu.VMEM((seqs, 3, hd, hh), F32),
                pltpu.VMEM((seqs, max(steps, 1), 3, hd, hh), BF16),
                pltpu.VMEM((seqs, max(steps, 1), 3, hd, hh), BF16),
                pltpu.VMEM((3, hd, hh), BF16),
                sem((2, 3 + seqs)),
                sem((3,)),
                sem((3, seqs)),
                sem((3, seqs, members)),
                sem((3, seqs, members)),
                sem((heads, seqs, n_head)),
                sem((heads, seqs, n_head)),
                sem((seqs, max(steps, 1))),
                sem((seqs, max(steps, 1))),
                sem((seqs, members, n_head)),
                sem((seqs, members, n_head)),
                sem((seqs, groups)),
            ],
            compiler_params=pltpu.CompilerParams(
                collective_id=0, has_side_effects=True, vmem_limit_bytes=60 * 1024 * 1024
            ),
            cost_estimate=pl.CostEstimate(
                flops=flops, bytes_accessed=queries.size * 8, transcendentals=0
            ),
        )(queries, first_keys, scaled, w_one, w_three, w_two, step_size, out_gain[None, :])

    return jax.shard_map(
        shards,
        mesh=mesh,
        in_specs=(
            P(None, None, "tok", "head"),
            P(None, "tok", "head"),
            P(None, "tok", "head"),
            P(None, "head", "tok"),
            P("head", None, None),
            P("head", None, None),
            P("head", None, None),
            P("head"),
            P(),
        ),
        out_specs=P(None, None, ("tok", "head"), None),
        check_vma=False,
    )
```

```python
import functools
import math

import jax
import jax.numpy as jnp
from jax import lax
from jax.experimental import pallas as pl
from jax.experimental.pallas import tpu as pltpu
from jax.sharding import PartitionSpec as P

MESH = pl.DeviceIdType.MESH
F32 = jnp.float32
BF16 = jnp.bfloat16


def dot(left, right):
    return jnp.dot(left, right, preferred_element_type=F32)


def dot_tn(left, right):
    return lax.dot_general(left, right, (((0,), (0,)), ((), ())), preferred_element_type=F32)


def dot_nt(left, right):
    return lax.dot_general(left, right, (((1,), (1,)), ((), ())), preferred_element_type=F32)


def fast_map(rows, one, three, two):
    gate = dot(rows, one)
    up = dot(rows, three)
    hidden = (gate * jax.nn.sigmoid(gate) * up).astype(BF16)
    return dot(hidden, two).astype(BF16)


def kernel(
    dims,
    queries, keys, values, w_one, w_three, w_two, step_size, rates,
    out,
    k_buf, s_buf, q_buf, v_buf, w_slot, x_slot, own_w, first_buf,
    acc, own, from_left, from_right, renewed,
    slot_sem, own_sem, v_sem, local_sem, tok_send, tok_recv, first_send, first_recv, first_local,
    right_send, right_recv, left_send, left_recv, second_send, second_recv, second_local,
):
    n_tok, n_head, seqs, heads, rows, hd, members = dims
    each = heads // members
    chunks = seqs * each
    units = 3 * chunks
    ranks = n_tok // members
    sub = rows // n_head
    tok, head = lax.axis_index("tok"), lax.axis_index("head")
    g = lax.rem(tok, members)
    base = tok - g
    rank = lax.div(tok, members)
    right = lax.rem(tok + members, n_tok)
    left = lax.rem(tok + n_tok - members, n_tok)

    def member(j):
        return lax.rem(g + j, members)

    def peer_head(k):
        return lax.rem(head + k, n_head)

    def cols(index):
        return pl.ds(pl.multiple_of(index * hd, hd), hd)

    def block(index):
        return pl.ds(pl.multiple_of(index * rows, rows), rows)

    barrier = pltpu.get_barrier_semaphore()
    count = 0
    for j in range(members):
        for k in range(n_head):
            if j or k:
                pl.semaphore_signal(
                    barrier, inc=1, device_id=(base + member(j), peer_head(k)), device_id_type=MESH
                )
                count += 1
    if ranks > 1:
        for side in (left, right):
            pl.semaphore_signal(barrier, inc=1, device_id=(side, head), device_id_type=MESH)
            count += 1

    own_copies = [
        pltpu.make_async_copy(w.at[pl.ds(g * each, each)], own_w.at[i], own_sem.at[i])
        for i, w in enumerate((w_one, w_three, w_two))
    ]
    value_copies = [
        pltpu.make_async_copy(values.at[s], v_buf.at[s], v_sem.at[s]) for s in range(seqs)
    ]
    for copy in value_copies:
        copy.start()
    pl.semaphore_wait(barrier, count)

    def token_parts(kind, c, peer):
        s, h = lax.div(c, each), peer * each + lax.rem(c, each)
        if kind == 0:
            source = keys.at[s, :, cols(h)]
        elif kind == 1:
            source = v_buf.at[s, :, cols(h)]
        else:
            source = queries.at[s, 1, :, cols(h)]
        return source, (k_buf, s_buf, q_buf)[kind].at[c, block(g), :]

    def token_copy(kind, c, j):
        peer = member(j)
        src, dst = token_parts(kind, c, peer)
        return pltpu.make_async_remote_copy(
            src_ref=src, dst_ref=dst,
            send_sem=tok_send.at[kind, c, j], recv_sem=tok_recv.at[kind, c, j],
            device_id=(base + peer, head), device_id_type=MESH,
        )

    def token_local(kind, c):
        src, dst = token_parts(kind, c, g)
        return pltpu.make_async_copy(src, dst, local_sem.at[kind, c])

    def scale(c, j):
        s, h = lax.div(c, each), member(j) * each + lax.rem(c, each)
        table = rates[s]
        lane = lax.broadcasted_iota(jnp.int32, table.shape, 1)
        rate = jnp.sum(jnp.where(lane == h, table, 0.0), axis=1, keepdims=True)
        v_buf[s, :, cols(h)] = (-rate * v_buf[s, :, cols(h)].astype(F32)).astype(BF16)

    for s in range(seqs):
        for e in range(each):
            c = jnp.int32(s * each + e)

            def send_keys(j, carry, c=c):
                token_copy(0, c, j).start()
                return carry

            lax.fori_loop(1, members, send_keys, 0)
            token_local(0, c).start()
            if e == 0:
                value_copies[s].wait()

            def send_scaled(j, carry, c=c):
                scale(c, j)
                token_copy(1, c, j).start()
                return carry

            lax.fori_loop(1, members, send_scaled, 0)
            scale(c, 0)
            token_local(1, c).start()
    for copy in own_copies:
        copy.start()

    def fetch(h, slot):
        copies = [
            pltpu.make_async_copy(w.at[h], w_slot.at[slot, i], slot_sem.at[slot, i])
            for i, w in enumerate((w_one, w_three, w_two))
        ]
        for s in range(seqs):
            copies.append(
                pltpu.make_async_copy(
                    queries.at[s, 0, :, cols(h)],
                    x_slot.at[slot, pl.ds(s * rows, rows), :],
                    slot_sem.at[slot, 3 + s],
                )
            )
        return copies

    def first_parts(h, s, dest):
        return (
            first_buf.at[h, pl.ds(pl.multiple_of(s * rows + dest * sub, sub), sub), :],
            out.at[s, 0, :, cols(head * heads + h)],
        )

    def first_copy(h, s, k):
        dest = peer_head(k)
        src, dst = first_parts(h, s, dest)
        return pltpu.make_async_remote_copy(
            src_ref=src, dst_ref=dst,
            send_sem=first_send.at[h, s, k], recv_sem=first_recv.at[h, s, k],
            device_id=(tok, dest), device_id_type=MESH,
        )

    def first_own(h, s):
        src, dst = first_parts(h, s, head)
        return pltpu.make_async_copy(src, dst, first_local.at[h, s])

    for copy in fetch(0, 0):
        copy.start()

    def first_body(h, carry):
        slot = lax.rem(h, 2)

        @pl.when(h + 1 < heads)
        def _():
            for copy in fetch(h + 1, lax.rem(h + 1, 2)):
                copy.start()

        for copy in fetch(h, slot):
            copy.wait()
        first_buf[h] = fast_map(x_slot[slot], w_slot[slot, 0], w_slot[slot, 1], w_slot[slot, 2])
        for s in range(seqs):
            for k in range(1, n_head):
                first_copy(h, s, k).start()
            first_own(h, s).start()
        return carry

    lax.fori_loop(0, heads, first_body, 0)
    for copy in own_copies:
        copy.wait()

    def add_block(c, b):
        e = lax.rem(c, each)
        key_rows = k_buf[c, block(b), :]
        scaled_rows = s_buf[c, block(b), :]
        gate = dot(key_rows, own_w[0, e])
        up = dot(key_rows, own_w[1, e])
        back = dot_nt(scaled_rows, own_w[2, e])
        sig = jax.nn.sigmoid(gate)
        swish = gate * sig
        hidden = (swish * up).astype(BF16)
        d_up = (back * swish).astype(BF16)
        d_gate = (back * up * sig * (1.0 + gate * (1.0 - sig))).astype(BF16)
        acc[0] += dot_tn(key_rows, d_gate)
        acc[1] += dot_tn(key_rows, d_up)
        acc[2] += dot_tn(hidden, scaled_rows)

    def gradients(c):
        acc[...] = jnp.zeros_like(acc)
        for kind in (0, 1):
            token_local(kind, c).wait()
        add_block(c, g)

        def body(j, carry):
            for kind in (0, 1):
                token_copy(kind, c, j).wait_recv()
            add_block(c, lax.rem(g + members - j, members))
            return carry

        lax.fori_loop(1, members, body, 0)
        for i in range(3):
            own[3 * c + i] = acc[i].astype(BF16)

        def send_queries(j, carry):
            token_copy(2, c, j).start()
            return carry

        lax.fori_loop(1, members, send_queries, 0)
        token_local(2, c).start()

    def right_copy(u):
        return pltpu.make_async_remote_copy(
            src_ref=from_left.at[u], dst_ref=from_left.at[u],
            send_sem=right_send.at[u], recv_sem=right_recv.at[u],
            device_id=(right, head), device_id_type=MESH,
        )

    def left_copy(u):
        return pltpu.make_async_remote_copy(
            src_ref=from_right.at[u], dst_ref=from_right.at[u],
            send_sem=left_send.at[u], recv_sem=left_recv.at[u],
            device_id=(left, head), device_id_type=MESH,
        )

    def pass_on(u, place, sums, copy):
        @pl.when(jnp.logical_and(u >= 0, u < units))
        def _():
            @pl.when(place == 0)
            def _():
                sums[u] = own[u]

            if ranks > 1:
                @pl.when(place > 0)
                def _():
                    copy(u).wait_recv()
                    sums[u] = (sums[u].astype(F32) + own[u].astype(F32)).astype(BF16)

                @pl.when(place < ranks - 1)
                def _():
                    copy(u).start()

    def second_parts(c, b, dest):
        h = head * heads + g * each + lax.rem(c, each)
        return (
            q_buf.at[c, pl.ds(pl.multiple_of(b * rows + dest * sub, sub), sub), :],
            out.at[lax.div(c, each), 1, :, cols(h)],
        )

    def second_copy(c, j, k):
        b, dest = member(j), peer_head(k)
        src, dst = second_parts(c, b, dest)
        return pltpu.make_async_remote_copy(
            src_ref=src, dst_ref=dst,
            send_sem=second_send.at[c, j, k], recv_sem=second_recv.at[c, j, k],
            device_id=(base + b, dest), device_id_type=MESH,
        )

    def second_own(c):
        src, dst = second_parts(c, g, head)
        return pltpu.make_async_copy(src, dst, second_local.at[c])

    def second(c):
        def map_block(b):
            q_buf[c, block(b), :] = fast_map(
                q_buf[c, block(b), :], renewed[0], renewed[1], renewed[2]
            )

        def body(j, carry):
            token_copy(2, c, j).wait_recv()
            b = lax.rem(g + members - j, members)
            map_block(b)
            for k in range(n_head):
                second_copy(c, lax.rem(members - j, members), k).start()
            return carry

        lax.fori_loop(1, members, body, 0)
        token_local(2, c).wait()
        map_block(g)
        for k in range(1, n_head):
            second_copy(c, 0, k).start()
        second_own(c).start()

    def renew(u):
        c, i = lax.div(u, 3), lax.rem(u, 3)
        e = lax.rem(c, each)
        total = from_left[u].astype(F32) + from_right[u].astype(F32) - own[u].astype(F32)
        mean_sq = jnp.mean(
            jnp.mean(total * total, axis=0, keepdims=True), axis=1, keepdims=True
        )
        factor = step_size[g * each + e] * lax.rsqrt(mean_sq + 1e-05)
        renewed[i] = (own_w[i, e].astype(F32) - factor * total).astype(BF16)

    def slot_body(t, carry):
        @pl.when(jnp.logical_and(lax.rem(t, 3) == 0, t < units))
        def _():
            gradients(lax.div(t, 3))

        pass_on(t - rank, rank, from_left, right_copy)
        pass_on(t - (ranks - 1 - rank), ranks - 1 - rank, from_right, left_copy)
        u = t - (ranks - 1)

        @pl.when(u >= 0)
        def _():
            renew(u)

            @pl.when(lax.rem(u, 3) == 2)
            def _():
                second(lax.div(u, 3))

        return carry

    lax.fori_loop(0, units + ranks - 1, slot_body, 0)

    def drain_first(h, carry):
        for s in range(seqs):
            for k in range(1, n_head):
                first_copy(h, s, k).wait()
            first_own(h, s).wait()
        return carry

    lax.fori_loop(0, heads, drain_first, 0)

    def drain_chunk(c, carry):
        for k in range(1, n_head):
            second_copy(c, 0, k).wait()
        second_own(c).wait()

        def drain_member(j, inner):
            for kind in range(3):
                token_copy(kind, c, j).wait_send()
            for k in range(n_head):
                second_copy(c, j, k).wait()
            return inner

        lax.fori_loop(1, members, drain_member, 0)
        return carry

    lax.fori_loop(0, chunks, drain_chunk, 0)

    if ranks > 1:
        def drain_sums(u, carry):
            @pl.when(rank < ranks - 1)
            def _():
                right_copy(u).wait_send()

            @pl.when(rank > 0)
            def _():
                left_copy(u).wait_send()

            return carry

        lax.fori_loop(0, units, drain_sums, 0)


def norm_kernel(block_rows, gain, normed):
    values = block_rows[...].astype(F32)
    mean_sq = jnp.mean(values * values, axis=-1, keepdims=True)
    normed[...] = (values * lax.rsqrt(mean_sq + 1e-06) * gain[...]).astype(BF16)


def solution(mesh):
    n_tok, n_head = mesh.shape["tok"], mesh.shape["head"]

    def shards(
        queries, first_keys, first_values, first_rates, w_one, w_three, w_two, step_size, out_gain
    ):
        seqs, groups, rows, here = queries.shape
        heads, hd, hh = w_one.shape
        members = math.gcd(4, heads, n_tok)
        each = heads // members
        chunks = seqs * each
        units = 3 * chunks
        sub = rows // n_head
        width = here * n_head
        rates = jnp.transpose(first_rates, (0, 2, 1))
        anywhere = pl.BlockSpec(memory_space=pl.ANY)
        vmem = pl.BlockSpec(memory_space=pltpu.VMEM)
        smem = pl.BlockSpec(memory_space=pltpu.SMEM)
        sem = pltpu.SemaphoreType.DMA
        dims = (n_tok, n_head, seqs, heads, rows, hd, members)
        tokens = (chunks, members * rows, hd)
        flops = 24 * seqs * heads * rows * hd * hh
        merged = pl.pallas_call(
            functools.partial(kernel, dims),
            out_shape=jax.ShapeDtypeStruct((seqs, groups, sub, width), BF16),
            in_specs=[anywhere] * 6 + [smem, vmem],
            out_specs=anywhere,
            scratch_shapes=[
                pltpu.VMEM(tokens, BF16),
                pltpu.VMEM(tokens, BF16),
                pltpu.VMEM(tokens, BF16),
                pltpu.VMEM((seqs, rows, here), BF16),
                pltpu.VMEM((2, 3, hd, hh), BF16),
                pltpu.VMEM((2, seqs * rows, hd), BF16),
                pltpu.VMEM((3, each, hd, hh), BF16),
                pltpu.VMEM((heads, seqs * rows, hd), BF16),
                pltpu.VMEM((3, hd, hh), F32),
                pltpu.VMEM((units, hd, hh), BF16),
                pltpu.VMEM((units, hd, hh), BF16),
                pltpu.VMEM((units, hd, hh), BF16),
                pltpu.VMEM((3, hd, hh), BF16),
                sem((2, 3 + seqs)),
                sem((3,)),
                sem((seqs,)),
                sem((3, chunks)),
                sem((3, chunks, members)),
                sem((3, chunks, members)),
                sem((heads, seqs, n_head)),
                sem((heads, seqs, n_head)),
                sem((heads, seqs)),
                sem((units,)),
                sem((units,)),
                sem((units,)),
                sem((units,)),
                sem((chunks, members, n_head)),
                sem((chunks, members, n_head)),
                sem((chunks,)),
            ],
            compiler_params=pltpu.CompilerParams(
                collective_id=0, has_side_effects=True, vmem_limit_bytes=60 * 1024 * 1024
            ),
            cost_estimate=pl.CostEstimate(
                flops=flops, bytes_accessed=queries.size * 8, transcendentals=0
            ),
        )(queries, first_keys, first_values, w_one, w_three, w_two, step_size, rates)
        all_rows = seqs * groups * sub
        tile = math.gcd(64, all_rows)
        normed = pl.pallas_call(
            norm_kernel,
            grid=(all_rows // tile,),
            out_shape=jax.ShapeDtypeStruct((all_rows, width), BF16),
            in_specs=[
                pl.BlockSpec((tile, width), lambda i: (i, 0)),
                pl.BlockSpec((1, width), lambda i: (0, 0)),
            ],
            out_specs=pl.BlockSpec((tile, width), lambda i: (i, 0)),
            compiler_params=pltpu.CompilerParams(vmem_limit_bytes=32 * 1024 * 1024),
        )(merged.reshape(all_rows, width), out_gain[None, :])
        return normed.reshape(merged.shape)

    return jax.shard_map(
        shards,
        mesh=mesh,
        in_specs=(
            P(None, None, "tok", "head"),
            P(None, "tok", "head"),
            P(None, "tok", "head"),
            P(None, "head", "tok"),
            P("head", None, None),
            P("head", None, None),
            P("head", None, None),
            P("head"),
            P(),
        ),
        out_specs=P(None, None, ("tok", "head"), None),
        check_vma=False,
    )
```

```python
import functools
import math

import jax
import jax.numpy as jnp
from jax import lax
from jax.experimental import pallas as pl
from jax.experimental.pallas import tpu as pltpu
from jax.sharding import PartitionSpec as P

MESH = pl.DeviceIdType.MESH
F32 = jnp.float32
BF16 = jnp.bfloat16
PIECES = 4
SKEW = 4


def dot(left, right):
    return jnp.dot(left, right, preferred_element_type=F32)


def dot_tn(left, right):
    return lax.dot_general(left, right, (((0,), (0,)), ((), ())), preferred_element_type=F32)


def dot_nt(left, right):
    return lax.dot_general(left, right, (((1,), (1,)), ((), ())), preferred_element_type=F32)


def fast_map(rows, one, three, two):
    gate = dot(rows, one)
    up = dot(rows, three)
    hidden = (gate * jax.nn.sigmoid(gate) * up).astype(BF16)
    return dot(hidden, two).astype(BF16)


def kernel(
    dims,
    queries, keys, values, w_one, w_three, w_two, step_size, rates,
    out,
    k_buf, s_buf, q_buf, v_buf, w_slot, x_slot, own_w, first_buf,
    acc, own, from_left, from_right, renewed,
    slot_sem, own_sem, v_sem, local_sem, tok_send, tok_recv, first_send, first_recv, first_local,
    right_send, right_recv, left_send, left_recv, second_send, second_recv, second_local,
):
    n_tok, n_head, seqs, heads, rows, hd, members = dims
    each = heads // members
    chunks = seqs * each
    span = 3 * PIECES
    units = span * chunks
    ranks = n_tok // members
    sub = rows // n_head
    tok, head = lax.axis_index("tok"), lax.axis_index("head")
    g = lax.rem(tok, members)
    base = tok - g
    rank = lax.div(tok, members)
    right = lax.rem(tok + members, n_tok)
    left = lax.rem(tok + n_tok - members, n_tok)

    def member(j):
        return lax.rem(g + j, members)

    def peer_head(k):
        return lax.rem(head + k, n_head)

    def cols(index):
        return pl.ds(pl.multiple_of(index * hd, hd), hd)

    def block(index):
        return pl.ds(pl.multiple_of(index * rows, rows), rows)

    barrier = pltpu.get_barrier_semaphore()
    count = 0
    for j in range(members):
        for k in range(n_head):
            if j or k:
                pl.semaphore_signal(
                    barrier, inc=1, device_id=(base + member(j), peer_head(k)), device_id_type=MESH
                )
                count += 1
    if ranks > 1:
        for side in (left, right):
            pl.semaphore_signal(barrier, inc=1, device_id=(side, head), device_id_type=MESH)
            count += 1

    own_copies = [
        pltpu.make_async_copy(w.at[pl.ds(g * each, each)], own_w.at[i], own_sem.at[i])
        for i, w in enumerate((w_one, w_three, w_two))
    ]
    value_copies = [
        pltpu.make_async_copy(values.at[s], v_buf.at[s], v_sem.at[s]) for s in range(seqs)
    ]
    for copy in value_copies:
        copy.start()
    pl.semaphore_wait(barrier, count)

    def token_parts(kind, c, peer):
        s, h = lax.div(c, each), peer * each + lax.rem(c, each)
        if kind == 0:
            source = keys.at[s, :, cols(h)]
        elif kind == 1:
            source = v_buf.at[s, :, cols(h)]
        else:
            source = queries.at[s, 1, :, cols(h)]
        return source, (k_buf, s_buf, q_buf)[kind].at[c, block(g), :]

    def token_copy(kind, c, j):
        peer = member(j)
        src, dst = token_parts(kind, c, peer)
        return pltpu.make_async_remote_copy(
            src_ref=src, dst_ref=dst,
            send_sem=tok_send.at[kind, c, j], recv_sem=tok_recv.at[kind, c, j],
            device_id=(base + peer, head), device_id_type=MESH,
        )

    def token_local(kind, c):
        src, dst = token_parts(kind, c, g)
        return pltpu.make_async_copy(src, dst, local_sem.at[kind, c])

    def scale(c, j):
        s, h = lax.div(c, each), member(j) * each + lax.rem(c, each)
        table = rates[s]
        lane = lax.broadcasted_iota(jnp.int32, table.shape, 1)
        rate = jnp.sum(jnp.where(lane == h, table, 0.0), axis=1, keepdims=True)
        v_buf[s, :, cols(h)] = (-rate * v_buf[s, :, cols(h)].astype(F32)).astype(BF16)

    def start_tokens(kind, c):
        def body(j, carry):
            token_copy(kind, c, j).start()
            return carry

        lax.fori_loop(1, members, body, 0)
        token_local(kind, c).start()

    ahead = min(2, chunks)
    for s in range(seqs):
        for e in range(each):
            c = jnp.int32(s * each + e)
            early = s * each + e < ahead
            if early:
                start_tokens(0, c)
            if e == 0:
                value_copies[s].wait()

            def scale_all(j, carry, c=c):
                scale(c, j)
                return carry

            lax.fori_loop(0, members, scale_all, 0)
            if early:
                start_tokens(1, c)
    for copy in own_copies:
        copy.start()

    def fetch(h, slot):
        copies = [
            pltpu.make_async_copy(w.at[h], w_slot.at[slot, i], slot_sem.at[slot, i])
            for i, w in enumerate((w_one, w_three, w_two))
        ]
        for s in range(seqs):
            copies.append(
                pltpu.make_async_copy(
                    queries.at[s, 0, :, cols(h)],
                    x_slot.at[slot, pl.ds(s * rows, rows), :],
                    slot_sem.at[slot, 3 + s],
                )
            )
        return copies

    def first_parts(h, s, dest):
        return (
            first_buf.at[h, pl.ds(pl.multiple_of(s * rows + dest * sub, sub), sub), :],
            out.at[s, 0, :, cols(head * heads + h)],
        )

    def first_copy(h, s, k):
        dest = peer_head(k)
        src, dst = first_parts(h, s, dest)
        return pltpu.make_async_remote_copy(
            src_ref=src, dst_ref=dst,
            send_sem=first_send.at[h, s, k], recv_sem=first_recv.at[h, s, k],
            device_id=(tok, dest), device_id_type=MESH,
        )

    def first_own(h, s):
        src, dst = first_parts(h, s, head)
        return pltpu.make_async_copy(src, dst, first_local.at[h, s])

    for copy in fetch(0, 0):
        copy.start()

    def first_body(h, carry):
        slot = lax.rem(h, 2)

        @pl.when(h + 1 < heads)
        def _():
            for copy in fetch(h + 1, lax.rem(h + 1, 2)):
                copy.start()

        for copy in fetch(h, slot):
            copy.wait()
        first_buf[h] = fast_map(x_slot[slot], w_slot[slot, 0], w_slot[slot, 1], w_slot[slot, 2])
        for s in range(seqs):
            for k in range(1, n_head):
                first_copy(h, s, k).start()
            first_own(h, s).start()
        return carry

    upfront = (heads + 1) // 2
    lax.fori_loop(0, upfront, first_body, 0)
    for copy in own_copies:
        copy.wait()

    def add_block(c, b):
        e = lax.rem(c, each)
        key_rows = k_buf[c, block(b), :]
        scaled_rows = s_buf[c, block(b), :]
        gate = dot(key_rows, own_w[0, e])
        up = dot(key_rows, own_w[1, e])
        back = dot_nt(scaled_rows, own_w[2, e])
        sig = jax.nn.sigmoid(gate)
        swish = gate * sig
        hidden = (swish * up).astype(BF16)
        d_up = (back * swish).astype(BF16)
        d_gate = (back * up * sig * (1.0 + gate * (1.0 - sig))).astype(BF16)
        acc[0] += dot_tn(key_rows, d_gate)
        acc[1] += dot_tn(key_rows, d_up)
        acc[2] += dot_tn(hidden, scaled_rows)

    def gradients(c):
        acc[...] = jnp.zeros_like(acc)
        for kind in (0, 1):
            token_local(kind, c).wait()
        add_block(c, g)

        def body(j, carry):
            for kind in (0, 1):
                token_copy(kind, c, j).wait_recv()
            add_block(c, lax.rem(g + members - j, members))
            return carry

        lax.fori_loop(1, members, body, 0)
        for i in range(3):
            own[pl.ds((3 * c + i) * PIECES, PIECES)] = (
                acc[i].astype(BF16).reshape(PIECES, hd // PIECES, acc.shape[-1])
            )

        @pl.when(c + ahead < chunks)
        def _():
            for kind in (0, 1):
                start_tokens(kind, c + ahead)

        start_tokens(2, c)

    def right_copy(u):
        return pltpu.make_async_remote_copy(
            src_ref=from_left.at[u], dst_ref=from_left.at[u],
            send_sem=right_send.at[u], recv_sem=right_recv.at[u],
            device_id=(right, head), device_id_type=MESH,
        )

    def left_copy(u):
        return pltpu.make_async_remote_copy(
            src_ref=from_right.at[u], dst_ref=from_right.at[u],
            send_sem=left_send.at[u], recv_sem=left_recv.at[u],
            device_id=(left, head), device_id_type=MESH,
        )

    def pass_on(u, place, sums, copy):
        @pl.when(jnp.logical_and(u >= 0, u < units))
        def _():
            @pl.when(place == 0)
            def _():
                sums[u] = own[u]

            if ranks > 1:
                @pl.when(place > 0)
                def _():
                    copy(u).wait_recv()
                    sums[u] = (sums[u].astype(F32) + own[u].astype(F32)).astype(BF16)

                @pl.when(place < ranks - 1)
                def _():
                    copy(u).start()

    def second_parts(c, b, dest):
        h = head * heads + g * each + lax.rem(c, each)
        return (
            q_buf.at[c, pl.ds(pl.multiple_of(b * rows + dest * sub, sub), sub), :],
            out.at[lax.div(c, each), 1, :, cols(h)],
        )

    def second_copy(c, j, k):
        b, dest = member(j), peer_head(k)
        src, dst = second_parts(c, b, dest)
        return pltpu.make_async_remote_copy(
            src_ref=src, dst_ref=dst,
            send_sem=second_send.at[c, j, k], recv_sem=second_recv.at[c, j, k],
            device_id=(base + b, dest), device_id_type=MESH,
        )

    def second_own(c):
        src, dst = second_parts(c, g, head)
        return pltpu.make_async_copy(src, dst, second_local.at[c])

    def second(c):
        def map_block(b):
            q_buf[c, block(b), :] = fast_map(
                q_buf[c, block(b), :], renewed[0], renewed[1], renewed[2]
            )

        def body(j, carry):
            token_copy(2, c, j).wait_recv()
            b = lax.rem(g + members - j, members)
            map_block(b)
            for k in range(n_head):
                second_copy(c, lax.rem(members - j, members), k).start()
            return carry

        lax.fori_loop(1, members, body, 0)
        token_local(2, c).wait()
        map_block(g)
        for k in range(1, n_head):
            second_copy(c, 0, k).start()
        second_own(c).start()

    def renew(matrix):
        c, i = lax.div(matrix, 3), lax.rem(matrix, 3)
        e = lax.rem(c, each)
        parts = pl.ds(matrix * PIECES, PIECES)
        total = (
            from_left[parts].astype(F32) + from_right[parts].astype(F32) - own[parts].astype(F32)
        ).reshape(acc.shape[1:])
        mean_sq = jnp.mean(
            jnp.mean(total * total, axis=0, keepdims=True), axis=1, keepdims=True
        )
        factor = step_size[g * each + e] * lax.rsqrt(mean_sq + 1e-05)
        renewed[i] = (own_w[i, e].astype(F32) - factor * total).astype(BF16)

    gradients(jnp.int32(0))
    lead = 4

    def slot_body(t, carry):
        pass_on(t - SKEW * rank, rank, from_left, right_copy)
        pass_on(t - SKEW * (ranks - 1 - rank), ranks - 1 - rank, from_right, left_copy)
        u = t - SKEW * (ranks - 1)

        @pl.when(jnp.logical_and(u >= 0, lax.rem(u, PIECES) == PIECES - 1))
        def _():
            renew(lax.div(u, PIECES))

            @pl.when(lax.rem(u, span) == span - 1)
            def _():
                second(lax.div(u, span))

        h = upfront + lax.div(t, 2)

        @pl.when(jnp.logical_and(lax.rem(t, 2) == 0, h < heads))
        def _():
            first_body(h, 0)

        later = t + lead

        @pl.when(jnp.logical_and(lax.rem(later, span) == 0, later < units))
        def _():
            gradients(lax.div(later, span))

        return carry

    lax.fori_loop(0, units + SKEW * (ranks - 1), slot_body, 0)

    def drain_first(h, carry):
        for s in range(seqs):
            for k in range(1, n_head):
                first_copy(h, s, k).wait()
            first_own(h, s).wait()
        return carry

    lax.fori_loop(0, heads, drain_first, 0)

    def drain_chunk(c, carry):
        for k in range(1, n_head):
            second_copy(c, 0, k).wait()
        second_own(c).wait()

        def drain_member(j, inner):
            for kind in range(3):
                token_copy(kind, c, j).wait_send()
            for k in range(n_head):
                second_copy(c, j, k).wait()
            return inner

        lax.fori_loop(1, members, drain_member, 0)
        return carry

    lax.fori_loop(0, chunks, drain_chunk, 0)

    if ranks > 1:
        def drain_sums(u, carry):
            @pl.when(rank < ranks - 1)
            def _():
                right_copy(u).wait_send()

            @pl.when(rank > 0)
            def _():
                left_copy(u).wait_send()

            return carry

        lax.fori_loop(0, units, drain_sums, 0)


def norm_kernel(block_rows, gain, normed):
    values = block_rows[...].astype(F32)
    mean_sq = jnp.mean(values * values, axis=-1, keepdims=True)
    normed[...] = (values * lax.rsqrt(mean_sq + 1e-06) * gain[...]).astype(BF16)


def solution(mesh):
    n_tok, n_head = mesh.shape["tok"], mesh.shape["head"]

    def shards(
        queries, first_keys, first_values, first_rates, w_one, w_three, w_two, step_size, out_gain
    ):
        seqs, groups, rows, here = queries.shape
        heads, hd, hh = w_one.shape
        members = math.gcd(4, heads, n_tok)
        each = heads // members
        chunks = seqs * each
        units = 3 * PIECES * chunks
        sub = rows // n_head
        width = here * n_head
        rates = jnp.transpose(first_rates, (0, 2, 1))
        anywhere = pl.BlockSpec(memory_space=pl.ANY)
        vmem = pl.BlockSpec(memory_space=pltpu.VMEM)
        smem = pl.BlockSpec(memory_space=pltpu.SMEM)
        sem = pltpu.SemaphoreType.DMA
        dims = (n_tok, n_head, seqs, heads, rows, hd, members)
        tokens = (chunks, members * rows, hd)
        flops = 24 * seqs * heads * rows * hd * hh
        merged = pl.pallas_call(
            functools.partial(kernel, dims),
            out_shape=jax.ShapeDtypeStruct((seqs, groups, sub, width), BF16),
            in_specs=[anywhere] * 6 + [smem, vmem],
            out_specs=anywhere,
            scratch_shapes=[
                pltpu.VMEM(tokens, BF16),
                pltpu.VMEM(tokens, BF16),
                pltpu.VMEM(tokens, BF16),
                pltpu.VMEM((seqs, rows, here), BF16),
                pltpu.VMEM((2, 3, hd, hh), BF16),
                pltpu.VMEM((2, seqs * rows, hd), BF16),
                pltpu.VMEM((3, each, hd, hh), BF16),
                pltpu.VMEM((heads, seqs * rows, hd), BF16),
                pltpu.VMEM((3, hd, hh), F32),
                pltpu.VMEM((units, hd // PIECES, hh), BF16),
                pltpu.VMEM((units, hd // PIECES, hh), BF16),
                pltpu.VMEM((units, hd // PIECES, hh), BF16),
                pltpu.VMEM((3, hd, hh), BF16),
                sem((2, 3 + seqs)),
                sem((3,)),
                sem((seqs,)),
                sem((3, chunks)),
                sem((3, chunks, members)),
                sem((3, chunks, members)),
                sem((heads, seqs, n_head)),
                sem((heads, seqs, n_head)),
                sem((heads, seqs)),
                sem((units,)),
                sem((units,)),
                sem((units,)),
                sem((units,)),
                sem((chunks, members, n_head)),
                sem((chunks, members, n_head)),
                sem((chunks,)),
            ],
            compiler_params=pltpu.CompilerParams(
                collective_id=0, has_side_effects=True, vmem_limit_bytes=60 * 1024 * 1024
            ),
            cost_estimate=pl.CostEstimate(
                flops=flops, bytes_accessed=queries.size * 8, transcendentals=0
            ),
        )(queries, first_keys, first_values, w_one, w_three, w_two, step_size, rates)
        all_rows = seqs * groups * sub
        tile = math.gcd(64, all_rows)
        normed = pl.pallas_call(
            norm_kernel,
            grid=(all_rows // tile,),
            out_shape=jax.ShapeDtypeStruct((all_rows, width), BF16),
            in_specs=[
                pl.BlockSpec((tile, width), lambda i: (i, 0)),
                pl.BlockSpec((1, width), lambda i: (0, 0)),
            ],
            out_specs=pl.BlockSpec((tile, width), lambda i: (i, 0)),
            compiler_params=pltpu.CompilerParams(vmem_limit_bytes=60 * 1024 * 1024),
        )(merged.reshape(all_rows, width), out_gain[None, :])
        return normed.reshape(merged.shape)

    return jax.shard_map(
        shards,
        mesh=mesh,
        in_specs=(
            P(None, None, "tok", "head"),
            P(None, "tok", "head"),
            P(None, "tok", "head"),
            P(None, "head", "tok"),
            P("head", None, None),
            P("head", None, None),
            P("head", None, None),
            P("head"),
            P(),
        ),
        out_specs=P(None, None, ("tok", "head"), None),
        check_vma=False,
    )
```
